32 devices in a mesh: rows: 8 (over z, x), piv: 4 (over y, core).
Axes of the slice: x: 2, y: 2, z: 4, core: 2. Of those that a mesh axis runs over, the one named last changes fastest.
Arguments:
- ancestor_sol: float32 [1024, 8192], P('piv', 'rows'), may hold values from -6 to 6
- front_map: int32 [64], P('rows'), may hold values from 0 to 63, each once
- lower_panel: float32 [8192, 12288], P('rows', 'piv'), may hold values from -0.0625 to 0.0625
- inverse_factor: float32 [12288, 12288], P('piv', 'rows'), as said below
- right_side: float32 [1024, 12288], P(None, ('piv', 'rows')), may hold values from -6 to 6
- child_start: int32 [32], P('rows'), may hold values from 0 to 12287, as said below
- child_len: int32 [32], P('rows'), may hold values from 1 to 128, as said below
Outputs:
- child_blocks: float32 [1024, 4096], P('piv', 'rows')
The draws below stay inside these ranges and needn't reach their ends.
Inputs may be any that keep to these rules, and one draw needn't show every extreme that they name: Child block c lies within pivots k * 1536 to (k + 1) * 1536 - 1, with k = c // 4; child_start[c] + child_len[c] <= (k + 1) * 1536. `child_len`: child block 0 is full. inverse_factor is lower triangular with a diagonal in [0.5, 2].
All inputs are finite; a program needn't handle non-finite values.
Results may differ from the reference program's by a relative error of at most 0.000088.
Values sent between devices are 32-bit elements; how exact they have to be, the bound alone decides.
A program may use at most 128 MiB of HBM per device.

```python
import jax
import jax.numpy as jnp
from jax import lax

PIVOTS = 12288
SOURCES = 1024
ROW_BLK = 128
CHILD_BLK = 128
CB_DEV = 4
NFB = 64
BOUNDARY = 8192
NCB = 32
PIV_ROWS = 1536


def child_pair(key):
    base = jax.random.fold_in(key, 4242)
    first, second = jax.random.split(base)
    lowest = CHILD_BLK // 4 + 1
    lengths = jax.random.randint(first, (NCB,), lowest, CHILD_BLK + 1).astype(jnp.int32)
    lengths = lengths.at[0].set(CHILD_BLK)
    owner = jnp.arange(NCB, dtype=jnp.int32) // CB_DEV
    room = PIV_ROWS - lengths + 1
    offset = jax.random.randint(second, (NCB,), 0, 1 << 20).astype(jnp.int32) % room
    return (owner * PIV_ROWS + offset, lengths)


def draw_child_start(key, part):
    return child_pair(key)[0]


def draw_child_len(key, part):
    return child_pair(key)[1]


def draw_inverse_factor(key, part):
    first, second = jax.random.split(jax.random.fold_in(key, 77))
    rowpos = jnp.arange(PIVOTS)[:, None]
    colpos = jnp.arange(PIVOTS)[None, :]
    values = jax.random.normal(first, (PIVOTS, PIVOTS), jnp.float32) * PIVOTS ** (-0.5)
    diagonal = jax.random.uniform(second, (PIVOTS,), jnp.float32, 0.5, 2.0)
    lower = jnp.where(rowpos > colpos, values, jnp.zeros_like(values))
    return lower + jnp.diag(diagonal)


def steps_of(own_key, extent, cuts, least, top_value):
    factor_of = 1.0
    for dim, shards_of in cuts:
        heights = jax.random.uniform(jax.random.fold_in(jax.random.fold_in(own_key, 6), dim), (shards_of,), jnp.float32, least / len(cuts), top_value / len(cuts))
        factor_of = factor_of * jnp.repeat(jnp.exp(heights), extent[dim] // shards_of).reshape((-1,) + (1,) * (len(extent) - 1 - dim))
    return factor_of


def bell_draw(stream_key, extent, deviation, reach, cuts=(), kind=jnp.bfloat16):
    entries = deviation * jax.random.normal(stream_key, extent, jnp.float32)
    if cuts:
        entries = entries * steps_of(stream_key, extent, cuts, -0.22, 0.18)
    return jnp.clip(entries, -reach, reach).astype(kind)


def setup_inputs(seed: int = 0) -> dict:
    key_list = jax.random.split(jax.random.key(seed), 8)
    return {
        "ancestor_sol": bell_draw(key_list[0], (SOURCES, BOUNDARY), 1.0, 6.0, ((0, 4), (1, 8)), jnp.float32),
        "front_map": jax.random.permutation(key_list[1], NFB).astype(jnp.int32),
        "lower_panel": bell_draw(key_list[2], (BOUNDARY, PIVOTS), BOUNDARY ** -0.5, 0.0625, ((0, 8), (1, 4)), jnp.float32),
        "inverse_factor": draw_inverse_factor(jax.random.fold_in(key_list[7], 71), 0),
        "right_side": bell_draw(key_list[4], (SOURCES, PIVOTS), 1.0, 6.0, ((1, 32),), jnp.float32),
        "child_start": draw_child_start(jax.random.fold_in(key_list[7], 71), 0),
        "child_len": draw_child_len(jax.random.fold_in(key_list[7], 71), 0),
    }


def reference(ancestor_sol, front_map, lower_panel, inverse_factor, right_side, child_start, child_len):
    blocks = ancestor_sol.reshape(SOURCES, NFB, ROW_BLK)
    boundary = jnp.take(blocks, front_map.astype(jnp.int32), axis=1).reshape(SOURCES, NFB * ROW_BLK)
    coupled = jnp.dot(boundary, lower_panel, precision=lax.Precision.HIGHEST, preferred_element_type=jnp.float32)
    reduced = right_side - coupled
    solution = jnp.dot(reduced, inverse_factor, precision=lax.Precision.HIGHEST, preferred_element_type=jnp.float32)
    slots = jnp.arange(CHILD_BLK, dtype=jnp.int32)
    index = child_start.astype(jnp.int32)[:, None] + slots[None, :]
    valid = slots[None, :] < child_len.astype(jnp.int32)[:, None]
    index = jnp.clip(index, 0, PIVOTS - 1).reshape(-1)
    picked = jnp.take(solution, index, axis=1)
    return jnp.where(valid.reshape(-1)[None, :], picked, jnp.zeros_like(picked))
```

```python
import functools

import jax
import jax.numpy as jnp
from jax import lax
from jax.experimental import pallas as pl
from jax.experimental.pallas import tpu as pltpu
from jax.sharding import PartitionSpec as P

ROW_BLK = 128
CHILD_BLK = 128


def reorder_kernel(map_ref, x_ref, o_ref):
    def move(j, carry):
        src = pl.multiple_of(map_ref[j] * ROW_BLK, ROW_BLK)
        dst = pl.multiple_of(j * ROW_BLK, ROW_BLK)
        o_ref[:, pl.ds(dst, ROW_BLK)] = x_ref[:, pl.ds(src, ROW_BLK)]
        return carry

    lax.fori_loop(0, map_ref.shape[0], move, 0)


def reorder(blocks, front):
    return pl.pallas_call(
        reorder_kernel,
        out_shape=jax.ShapeDtypeStruct(blocks.shape, blocks.dtype),
        in_specs=[
            pl.BlockSpec(memory_space=pltpu.SMEM),
            pl.BlockSpec(memory_space=pltpu.VMEM),
        ],
        out_specs=pl.BlockSpec(memory_space=pltpu.VMEM),
        compiler_params=pltpu.CompilerParams(vmem_limit_bytes=16 * 2**20),
    )(front, blocks)


def dot(a, b):
    return jnp.dot(a, b, precision=lax.Precision.HIGH, preferred_element_type=jnp.float32)


def pick_columns(inverse_factor, child_start, child_len, first):
    span = inverse_factor.shape[1]
    slots = jnp.arange(CHILD_BLK, dtype=jnp.int32)[None, :]
    parts = []
    for c in range(child_start.shape[0]):
        start = child_start[c] - first
        base = jnp.clip(start, 0, span - CHILD_BLK)
        shift = jnp.clip(start - base, 0, CHILD_BLK)
        taken = lax.dynamic_slice_in_dim(inverse_factor, base, CHILD_BLK, 1)
        taken = jnp.concatenate([taken, jnp.zeros_like(taken)], axis=1)
        taken = lax.dynamic_slice_in_dim(taken, shift, CHILD_BLK, 1)
        parts.append(jnp.where(slots < child_len[c], taken, 0.0))
    return jnp.concatenate(parts, axis=1)


def body(n, ancestor_sol, front_map, lower_panel, inverse_factor, right_side, child_start, child_len):
    me = lax.axis_index("rows")
    half = n // 2
    order = [2 * i for i in range(half)] + [2 * i + 1 for i in reversed(range(half))]
    pos = jnp.where(me % 2 == 0, me // 2, n - 1 - me // 2)
    up = [(order[i], order[(i + 1) % n]) for i in range(n)]
    down = [(order[(i + 1) % n], order[i]) for i in range(n)]

    front = lax.all_gather(front_map, "rows", axis=0, tiled=True)
    spread = lax.all_to_all(ancestor_sol, "rows", split_axis=0, concat_axis=1, tiled=True)
    mine = lax.all_to_all(reorder(spread, front), "rows", split_axis=1, concat_axis=0, tiled=True)
    boundary = lax.all_gather(mine, "piv", axis=0, tiled=True)

    sources = boundary.shape[0]
    piece = sources // n
    cut = piece // 2
    width = lower_panel.shape[1]
    own_cols = right_side.shape[1]

    def source_piece(array, off):
        return lax.dynamic_slice_in_dim(array, ((pos + off) % n) * piece, piece, 0)

    partial = {}

    def make(offs):
        rows = jnp.concatenate([source_piece(boundary, o) for o in offs], axis=0)
        rhs = jnp.concatenate([source_piece(right_side, o) for o in offs], axis=0)
        out = -dot(rows, lower_panel)
        old = lax.dynamic_slice_in_dim(out, me * own_cols, own_cols, 1)
        out = lax.dynamic_update_slice_in_dim(out, old + rhs, me * own_cols, 1)
        for i, o in enumerate(offs):
            partial[o] = out[i * piece : (i + 1) * piece]

    for k in range(1, half):
        make((n - k, k))
    make((half, 0))

    acc_up = partial[n - 1][:cut]
    acc_down = partial[1][cut:]
    for t in range(n - 1):
        acc_up = lax.ppermute(acc_up, "rows", up) + partial[(-2 - t) % n][:cut]
        acc_down = lax.ppermute(acc_down, "rows", down) + partial[(2 + t) % n][cut:]

    picked = pick_columns(inverse_factor, child_start, child_len, me * inverse_factor.shape[1])
    result = jnp.zeros((sources, picked.shape[1]), jnp.float32)

    def place(result, part, off, shift):
        return lax.dynamic_update_slice_in_dim(
            result, part, ((pos + off) % n) * piece + shift, 0
        )

    hold_up, hold_down = acc_up, acc_down
    for t in range(n):
        part = dot(jnp.concatenate([hold_up, hold_down], axis=0), picked)
        result = place(result, part[:cut], -t + n, 0)
        result = place(result, part[cut:], t, cut)
        if t < n - 1:
            hold_up = lax.ppermute(hold_up, "rows", up)
            hold_down = lax.ppermute(hold_down, "rows", down)
    return lax.psum_scatter(result, "piv", scatter_dimension=0, tiled=True)


def solution(mesh):
    placed = (
        P("piv", "rows"),
        P("rows"),
        P("rows", "piv"),
        P("piv", "rows"),
        P(None, ("piv", "rows")),
        P("rows"),
        P("rows"),
    )
    return jax.shard_map(
        functools.partial(body, mesh.shape["rows"]),
        mesh=mesh,
        in_specs=placed,
        out_specs=P("piv", "rows"),
        check_vma=False,
    )
```

```python
import functools

import jax
import jax.numpy as jnp
from jax import lax
from jax.experimental import pallas as pl
from jax.experimental.pallas import tpu as pltpu
from jax.sharding import PartitionSpec as P

ROW_BLK = 128
CHILD_BLK = 128
STREAMS = 2


def reorder_kernel(map_ref, x_ref, o_ref):
    def move(j, carry):
        src = pl.multiple_of(map_ref[j] * ROW_BLK, ROW_BLK)
        dst = pl.multiple_of(j * ROW_BLK, ROW_BLK)
        o_ref[:, pl.ds(dst, ROW_BLK)] = x_ref[:, pl.ds(src, ROW_BLK)]
        return carry

    lax.fori_loop(0, map_ref.shape[0], move, 0)


def reorder(blocks, front):
    return pl.pallas_call(
        reorder_kernel,
        out_shape=jax.ShapeDtypeStruct(blocks.shape, blocks.dtype),
        in_specs=[
            pl.BlockSpec(memory_space=pltpu.SMEM),
            pl.BlockSpec(memory_space=pltpu.VMEM),
        ],
        out_specs=pl.BlockSpec(memory_space=pltpu.VMEM),
        compiler_params=pltpu.CompilerParams(vmem_limit_bytes=16 * 2**20),
    )(front, blocks)


def dot(a, b):
    return jnp.dot(a, b, precision=lax.Precision.HIGH, preferred_element_type=jnp.float32)


def pick_columns(inverse_factor, child_start, child_len, first):
    span = inverse_factor.shape[1]
    slots = jnp.arange(CHILD_BLK, dtype=jnp.int32)[None, :]
    parts = []
    for c in range(child_start.shape[0]):
        start = child_start[c] - first
        base = jnp.clip(start, 0, span - CHILD_BLK)
        shift = jnp.clip(start - base, 0, CHILD_BLK)
        taken = lax.dynamic_slice_in_dim(inverse_factor, base, CHILD_BLK, 1)
        taken = jnp.concatenate([taken, jnp.zeros_like(taken)], axis=1)
        taken = lax.dynamic_slice_in_dim(taken, shift, CHILD_BLK, 1)
        parts.append(jnp.where(slots < child_len[c], taken, 0.0))
    return jnp.concatenate(parts, axis=1)


def gather_map(front_map, n, me):
    count = front_map.shape[0]
    whole = lax.dynamic_update_slice(
        jnp.zeros((n * count,), front_map.dtype), front_map, (me * count,)
    )
    for k in range(1, n):
        came = lax.ppermute(front_map, "rows", [(i, (i + k) % n) for i in range(n)])
        whole = lax.dynamic_update_slice(whole, came, (((me - k) % n) * count,))
    return whole


def scatter_sum(part, size, index):
    step = 1
    while step < size:
        bit = (index // step) % 2
        pairs = part.reshape((part.shape[0] // 2, 2) + part.shape[1:])
        keep = lax.dynamic_index_in_dim(pairs, bit, 1, keepdims=False)
        give = lax.dynamic_index_in_dim(pairs, 1 - bit, 1, keepdims=False)
        part = keep + lax.ppermute(give, "piv", [(i, i ^ step) for i in range(size)])
        step *= 2
    return part.reshape(part.shape[1:])


def body(n, groups, ancestor_sol, front_map, lower_panel, inverse_factor, right_side, child_start, child_len):
    me = lax.axis_index("rows")
    half = n // 2
    order = [2 * i for i in range(half)] + [2 * i + 1 for i in reversed(range(half))]
    pos = jnp.where(me % 2 == 0, me // 2, n - 1 - me // 2)
    up = [(order[i], order[(i + 1) % n]) for i in range(n)]
    down = [(order[(i + 1) % n], order[i]) for i in range(n)]

    local = ancestor_sol.shape[0]
    share = local // n
    cut = share // 2
    rows = groups * cut
    streams = range(STREAMS)
    slab = rows // STREAMS
    own_cols = right_side.shape[1]

    front = gather_map(front_map, n, me)
    spread = lax.all_to_all(ancestor_sol, "rows", split_axis=0, concat_axis=1, tiled=True)
    mine = lax.all_to_all(reorder(spread, front), "rows", split_axis=1, concat_axis=0, tiled=True)
    boundary = lax.all_gather(mine, "piv", axis=0, tiled=True)
    picked = pick_columns(inverse_factor, child_start, child_len, me * inverse_factor.shape[1])
    boundary, picked = lax.optimization_barrier((boundary, picked))
    boundary = boundary.reshape(groups, local, -1)
    sides = right_side.reshape(groups, local, own_cols)

    def first_row(off):
        return ((pos + off) % n) * share

    def source_piece(array, off):
        return [
            lax.dynamic_slice_in_dim(array, first_row(off) + d * cut, cut, 1).reshape(rows, -1)
            for d in range(2)
        ]

    partial = {}

    def make(offs):
        left = jnp.concatenate(sum([source_piece(boundary, o) for o in offs], []), axis=0)
        rhs = jnp.concatenate(sum([source_piece(sides, o) for o in offs], []), axis=0)
        out = -dot(left, lower_panel)
        old = lax.dynamic_slice_in_dim(out, me * own_cols, own_cols, 1)
        out = lax.dynamic_update_slice_in_dim(out, old + rhs, me * own_cols, 1)
        for i, o in enumerate(offs):
            partial[o] = out[2 * i * rows : 2 * (i + 1) * rows]

    for k in range(1, half):
        make((n - k, k))
    make((half, 0))

    def part_up(off, s):
        return partial[off % n][s * slab : (s + 1) * slab]

    def part_down(off, s):
        return partial[off % n][rows + s * slab : rows + (s + 1) * slab]

    hold_up = [part_up(-1, s) for s in streams]
    hold_down = [part_down(1, s) for s in streams]
    for t in range(n - 1):
        for s in streams:
            more_up, more_down = part_up(-2 - t, s), part_down(2 + t, s)
            if s:
                hold_up[s - 1], hold_down[s - 1], more_up, more_down = lax.optimization_barrier(
                    (hold_up[s - 1], hold_down[s - 1], more_up, more_down)
                )
            hold_up[s] = lax.ppermute(hold_up[s], "rows", up) + more_up
            hold_down[s] = lax.ppermute(hold_down[s], "rows", down) + more_down

    parts = []
    for t in range(n):
        now = list(hold_up + hold_down)
        if t < n - 1:
            for s in streams:
                hold_up[s] = lax.ppermute(hold_up[s], "rows", up)
                hold_down[s] = lax.ppermute(hold_down[s], "rows", down)
        part = dot(jnp.concatenate(now, axis=0), picked)
        part = part.reshape(2, groups, cut, -1).transpose(1, 0, 2, 3)
        parts.append(part.reshape(groups, 2 * cut, -1))
    total = scatter_sum(jnp.concatenate(parts, axis=1), groups, lax.axis_index("piv"))
    result = jnp.zeros((local, picked.shape[1]), jnp.float32)
    for t in range(n):
        part = total[t * share : (t + 1) * share]
        result = lax.dynamic_update_slice_in_dim(result, part[:cut], first_row(n - t), 0)
        result = lax.dynamic_update_slice_in_dim(result, part[cut:], first_row(t) + cut, 0)
    return result


def solution(mesh):
    placed = (
        P("piv", "rows"),
        P("rows"),
        P("rows", "piv"),
        P("piv", "rows"),
        P(None, ("piv", "rows")),
        P("rows"),
        P("rows"),
    )
    return jax.shard_map(
        functools.partial(body, mesh.shape["rows"], mesh.shape["piv"]),
        mesh=mesh,
        in_specs=placed,
        out_specs=P("piv", "rows"),
        check_vma=False,
    )
```
